32 devices in a mesh: dp: 8 (over z, y), seq: 4 (over x, core).
Axes of the slice: x: 2, y: 2, z: 4, core: 2. Of those that a mesh axis runs over, the one named last changes fastest.
Arguments:
- grad_out: bfloat16 [8, 512, 2560], P('dp', 'seq'), may hold values from -6 to 6
- branch_out: bfloat16 [8, 512, 2560], P('dp', 'seq'), may hold values from -0.59765625 to 0.59765625
- down_weight: bfloat16 [8192, 2560], P('seq', 'dp'), may hold values from -0.0625 to 0.0625
- mod_gate: float32 [2560], replicated, may hold values from -3 to 3
- level_table: float32 [64, 2560], replicated, may hold values from -3 to 3
- frame_ids: int32 [8, 512], P('dp', 'seq'), may hold values from 0 to 2, never falling along the last dimension, each value on 1 to 384 neighbouring positions
- levels: int32 [8, 3], P('dp'), may hold values from 0 to 63
Outputs:
- hidden_grad: bfloat16 [8, 512, 8192], P('dp', None, 'seq')
- frame_grad: float32 [8, 3, 2560], P('dp', None, 'seq')
- table_grad: float32 [64, 2560], P('dp', 'seq')
The draws below stay inside these ranges and needn't reach their ends.
Inputs may be any that keep to these rules, and one draw needn't show every extreme that they name: `frame_ids`: within each clip the frame ids never fall along the tokens; every frame holds 1 to 384 tokens, and some frame exactly 384.
All inputs are finite; a program needn't handle non-finite values.
Results may differ from the reference program's by a relative error of at most 0.0049.
Values may be sent and summed in bfloat16 or wider, within the bound.
No kernel may reach another device: no remote copies, remote signals or barrier semaphores. Data moves between devices by JAX's collectives and lax.ppermute only.
A program may use at most 128 MiB of HBM per device.

```python
import math
import jax
import jax.numpy as jnp
import numpy as np
from jax import lax

D = 2560
FF = 8192
TOK = 128
LEVELS = 64
FRAMES = 3
SLAB = 512
CLIPS = 8


def plant(array, rng, low, largest):
    extent = array.shape
    place = [jax.random.randint(jax.random.fold_in(rng, axis), (), 0, extent[axis]) for axis in range(len(extent))]
    array = array.at[tuple(place)].set(low)
    longest = extent.index(max(extent))
    place[longest] = (place[longest] + 1) % extent[longest]
    return array.at[tuple(place)].set(largest)


def steps_of(key, extent, shards, least, top_value):
    factor_of, own = 1.0, jax.random.fold_in(key, 6)
    for axis_at, parts in shards:
        steps = jnp.exp(jax.random.uniform(jax.random.fold_in(own, axis_at), (parts,), jnp.float32, least / len(shards), top_value / len(shards)))
        factor_of = factor_of * jnp.repeat(steps, extent[axis_at] // parts).reshape([-1 if axis == axis_at else 1 for axis in range(len(extent))])
    return factor_of


def split_up(amount, total, bound, skew):
    weights = [(1 << 20) // math.isqrt(rank ** skew) + 1 for rank in range(2, amount + 1)]
    surplus, holding = total - bound - (amount - 1), [1] * (amount - 1)
    while surplus > 0:
        movable = [i for i in range(amount - 1) if holding[i] < bound]
        whole, remaining = sum([weights[i] for i in movable]), surplus
        for i in movable:
            addition = min(bound - holding[i], max(1, remaining * weights[i] // whole), surplus)
            holding[i] = holding[i] + addition
            surplus = surplus - addition
    return np.array([bound] + holding)


def ragged_sizes(own_key, number_of, total, bound, skew):
    if number_of == 2:
        one = jax.random.randint(own_key, (), max(1, total - bound), min(bound, total - 1) + 1)
        return jnp.stack([one, total - one])
    sizes = jnp.asarray(split_up(number_of, total, bound, skew), jnp.int32)
    pairs = (number_of - 1) // 2
    source_of, sink = sizes[1:1 + 2 * pairs:2], sizes[2:2 + 2 * pairs:2]
    room = jnp.minimum(source_of - 1, bound - sink)
    shifted = jax.random.randint(jax.random.fold_in(own_key, 1), (pairs,), 0, 1 << 20) % (room + 1)
    sizes = sizes.at[1:1 + 2 * pairs:2].set(source_of - shifted).at[2:2 + 2 * pairs:2].set(sink + shifted)
    return sizes[jax.random.permutation(jax.random.fold_in(own_key, 2), number_of)]


def centred(stream_key, shape, scale, most, split=(), kind=jnp.bfloat16):
    values = scale * jax.random.normal(stream_key, shape, jnp.float32)
    if split:
        values = values * steps_of(stream_key, shape, split, -0.22, 0.18)
    return jnp.clip(values, -most, most).astype(kind)


def setup_inputs(seed: int = 0) -> dict:
    key_of = jax.random.split(jax.random.key(seed), 8)
    return {
        "grad_out": centred(key_of[0], (CLIPS, SLAB, D), 1.0, 6.0, ((0, 8), (1, 4))),
        "branch_out": centred(key_of[1], (CLIPS, SLAB, D), 0.1, 0.59765625, ((0, 8), (1, 4))),
        "down_weight": centred(key_of[2], (FF, D), FF ** -0.5, 0.0625, ((0, 4), (1, 8))),
        "mod_gate": centred(key_of[3], (D,), 0.5, 3.0, (), jnp.float32),
        "level_table": centred(key_of[4], (LEVELS, D), 0.5, 3.0, (), jnp.float32),
        "frame_ids": jax.vmap(lambda own: jnp.searchsorted(jnp.cumsum(ragged_sizes(own, FRAMES, SLAB, 3 * TOK, 2)), jnp.arange(SLAB), side="right"))(jax.random.split(key_of[5], CLIPS)).reshape((CLIPS, SLAB)).astype(jnp.int32),
        "levels": plant(jax.random.randint(key_of[6], (CLIPS, FRAMES), 0, LEVELS), jax.random.fold_in(key_of[6], 1), 0, LEVELS - 1).astype(jnp.int32),
    }


def reference(grad_out, branch_out, down_weight, mod_gate, level_table, frame_ids, levels):
    highest = lax.Precision.HIGHEST

    def one_clip(items):
        upstream, saved, token_frames, level_row = items
        frame_onehot = (token_frames[:, None] == jnp.arange(FRAMES, dtype=jnp.int32)[None, :]).astype(jnp.float32)
        level_onehot = (level_row[:, None] == jnp.arange(LEVELS, dtype=jnp.int32)[None, :]).astype(jnp.float32)
        gate_frames = mod_gate[None, :] + jnp.dot(level_onehot, level_table, precision=highest)
        gate_tokens = jnp.dot(frame_onehot, gate_frames, precision=highest)
        scaled = (gate_tokens * upstream.astype(jnp.float32)).astype(jnp.bfloat16)
        hidden = lax.dot_general(scaled, down_weight, (((1,), (1,)), ((), ())), preferred_element_type=jnp.float32).astype(jnp.bfloat16)
        products = upstream.astype(jnp.float32) * saved.astype(jnp.float32)
        frame_sum = jnp.dot(frame_onehot.T, products, precision=highest)
        level_part = jnp.dot(level_onehot.T, frame_sum, precision=highest)
        return hidden, frame_sum, level_part

    hidden_grad, frame_grad, level_parts = lax.map(one_clip, (grad_out, branch_out, frame_ids, levels))
    table_grad = jnp.sum(level_parts, axis=0)
    return hidden_grad, frame_grad, table_grad
```

```python
import jax
import jax.numpy as jnp
from jax import lax
from jax.experimental import pallas as pl
from jax.experimental.pallas import tpu as pltpu
from jax.sharding import PartitionSpec as P

HIGHEST = lax.Precision.HIGHEST
GROUPS = ((1,), (1, 1, 1))


def gate_and_products(grad_out, branch_out, mod_gate, level_table, frame_ids, levels):
    upstream = grad_out[0].astype(jnp.float32)
    saved = branch_out[0].astype(jnp.float32)
    frames = frame_ids[0]
    level_row = levels[0]
    frame_range = jnp.arange(level_row.shape[0], dtype=jnp.int32)
    level_range = jnp.arange(level_table.shape[0], dtype=jnp.int32)
    frame_onehot = (frames[:, None] == frame_range[None, :]).astype(jnp.float32)
    level_onehot = (level_row[:, None] == level_range[None, :]).astype(jnp.float32)
    gate_frames = mod_gate[None, :] + jnp.dot(level_onehot, level_table, precision=HIGHEST)
    gate_tokens = jnp.dot(frame_onehot, gate_frames, precision=HIGHEST)
    scaled = (gate_tokens * upstream).astype(jnp.bfloat16)
    frame_part = jnp.dot(frame_onehot.T, upstream * saved, precision=HIGHEST)
    return scaled, frame_part, level_onehot


def plain_body(grad_out, branch_out, down_weight, mod_gate, level_table, frame_ids, levels):
    scaled, frame_part, level_onehot = gate_and_products(
        grad_out, branch_out, mod_gate, level_table, frame_ids, levels
    )
    hidden_grad = lax.dot_general(
        lax.all_gather(scaled, "seq", axis=0, tiled=True),
        lax.all_gather(down_weight, "dp", axis=1, tiled=True),
        (((1,), (1,)), ((), ())),
        preferred_element_type=jnp.float32,
    ).astype(jnp.bfloat16)
    frame_grad = lax.psum_scatter(frame_part, "seq", scatter_dimension=1, tiled=True)
    level_part = jnp.dot(level_onehot.T, frame_grad, precision=HIGHEST)
    table_grad = lax.psum_scatter(level_part, "dp", scatter_dimension=0, tiled=True)
    return hidden_grad[None], frame_grad[None], table_grad


def seq_step(frame_part, seq, flip, gate):
    width = frame_part.shape[1] // 2
    low, high = frame_part[:, :width], frame_part[:, width:]
    upper = (lax.axis_index("seq") & flip) != 0
    sent = after(jnp.where(upper, low, high), *gate)
    held = jnp.where(upper, high, low)
    return held + lax.ppermute(sent, "seq", [(i, i ^ flip) for i in range(seq)])


def pack_frames(frame_grad, levels):
    frame_count, width = frame_grad.shape
    level_line = jnp.pad(levels.astype(jnp.float32), ((0, 0), (0, width - frame_count)))
    return jnp.concatenate([frame_grad, level_line], axis=0)[None]


def clip_step(packed, dp, flip, gate):
    sent = after(packed, *gate)
    arrived = lax.ppermute(sent, "dp", [(i, i ^ flip) for i in range(dp)])
    return jnp.concatenate([packed, arrived], axis=0)


def table_of(packed, level_count):
    dp, lines, width = packed.shape
    frame_count = lines - 1
    owned = level_count // dp
    rows = (lax.axis_index("dp") * owned + jnp.arange(owned, dtype=jnp.int32)).astype(jnp.float32)
    sums = packed[:, :frame_count].reshape(dp * frame_count, width)
    marks = packed[:, frame_count, :frame_count].reshape(dp * frame_count)
    onehot = (rows[:, None] == marks[None, :]).astype(jnp.float32)
    return jnp.dot(onehot, sums, precision=HIGHEST)


def after(array, *earlier):
    return lax.optimization_barrier((array, *earlier))[0]


def join_rows(first_row, upper, lower, offset):
    rows, width = upper.shape
    vmem = pl.BlockSpec(memory_space=pltpu.VMEM)

    def kernel(first_row, upper, lower, result):
        start = pl.multiple_of(first_row[0], 16)
        result[pl.ds(start, rows), :] = upper[...]
        rest = pl.multiple_of(rows - start, 16)
        result[pl.ds(rest, rows), :] = lower[:, offset : offset + width]

    return pl.pallas_call(
        kernel,
        out_shape=jax.ShapeDtypeStruct((2 * rows, width), upper.dtype),
        in_specs=[pl.BlockSpec(memory_space=pltpu.SMEM), vmem, vmem],
        out_specs=vmem,
        compiler_params=pltpu.CompilerParams(vmem_limit_bytes=16 << 20),
        name="join_rows",
    )(first_row.astype(jnp.int32).reshape(1), upper, lower)


def stack_rows(upper, lower, start, width):
    rows = upper.shape[0]
    vmem = pl.BlockSpec(memory_space=pltpu.VMEM)

    def kernel(upper, lower, result):
        result[:rows] = upper[:, start : start + width]
        result[rows:] = lower[:, start : start + width]

    return pl.pallas_call(
        kernel,
        out_shape=jax.ShapeDtypeStruct((2 * rows, width), upper.dtype),
        in_specs=[vmem, vmem],
        out_specs=vmem,
        compiler_params=pltpu.CompilerParams(vmem_limit_bytes=16 << 20),
        name="stack_rows",
    )(upper, lower)


def order_pieces(me, pieces):
    count = len(pieces)
    rows, width = pieces[0].shape
    any_space = pl.BlockSpec(memory_space=pl.ANY)

    def kernel(place, *refs):
        result, sems = refs[count], refs[count + 1]
        copies = []
        for flip in range(count):
            start = pl.multiple_of((place[0] ^ flip) * rows, 128)
            copies.append(
                pltpu.make_async_copy(refs[flip], result.at[pl.ds(start, rows)], sems.at[flip])
            )
            copies[-1].start()
        for copy in copies:
            copy.wait()

    return pl.pallas_call(
        kernel,
        out_shape=jax.ShapeDtypeStruct((count * rows, width), pieces[0].dtype),
        in_specs=[pl.BlockSpec(memory_space=pltpu.SMEM)] + [any_space] * count,
        out_specs=pl.BlockSpec(memory_space=pltpu.VMEM),
        scratch_shapes=[pltpu.SemaphoreType.DMA((count,))],
        compiler_params=pltpu.CompilerParams(vmem_limit_bytes=16 << 20),
        name="order_pieces",
    )(me.astype(jnp.int32).reshape(1), *pieces)


def assemble(y, starts, kept, received):
    count, half = len(kept), sum(part.shape[1] for part in kept)
    rows = kept[0].shape[0]
    vmem = pl.BlockSpec(memory_space=pltpu.VMEM)

    def kernel(place, *refs):
        result = refs[2 * count]
        for index, start in enumerate(starts):
            width = kept[index].shape[1]
            mine = pl.multiple_of(place[0] * half + start, 128)
            theirs = pl.multiple_of((1 - place[0]) * half + start, 128)
            result[:, pl.ds(mine, width)] = refs[index][...]
            result[:, pl.ds(theirs, width)] = refs[count + index][...]

    return pl.pallas_call(
        kernel,
        out_shape=jax.ShapeDtypeStruct((rows, 2 * half), kept[0].dtype),
        in_specs=[pl.BlockSpec(memory_space=pltpu.SMEM)] + [vmem] * (2 * count),
        out_specs=vmem,
        compiler_params=pltpu.CompilerParams(vmem_limit_bytes=16 << 20),
        name="assemble",
    )(y.astype(jnp.int32).reshape(1), *kept, *received)


def staged_body(grad_out, branch_out, down_weight, mod_gate, level_table, frame_ids, levels):
    dp, seq = 8, 4
    clip, me = lax.axis_index("dp"), lax.axis_index("seq")
    z, y = clip // 2, clip % 2
    is_mid = jnp.logical_or(z == 1, z == 2)
    hidden, shard = down_weight.shape
    half = hidden // 2
    block = 2 * shard

    def along_z(array, pairs):
        perm = [(a * 2 + s, b * 2 + s) for a, b in pairs for s in range(2)]
        return lax.ppermute(array, "dp", perm)

    def over_y(array):
        return lax.ppermute(array, "dp", [(i, i ^ 1) for i in range(dp)])

    def over_seq(array, flip):
        return lax.ppermute(array, "seq", [(i, i ^ flip) for i in range(seq)])

    def ordered(flag, first, second, axis):
        swapped = jnp.concatenate([second, first], axis=axis)
        return jnp.where(flag, swapped, jnp.concatenate([first, second], axis=axis))

    weight = down_weight.T
    unit = half // sum(sum(group) for group in GROUPS)
    starts, start = [], 0
    for group in GROUPS:
        starts.append(start)
        start += sum(group) * unit

    def columns(owner, start, width):
        return lax.dynamic_slice(weight, (0, owner * half + start), (shard, width))

    def own_block(index, arrived, offset):
        width = sum(GROUPS[index]) * unit
        return join_rows(y * shard, columns(y, starts[index], width), arrived, offset)

    def pairs_of(index, own, near):
        blocks, offset = [], 0
        for width in GROUPS[index]:
            blocks.append((starts[index] + offset, stack_rows(own, near, offset, width * unit)))
            offset += width * unit
        return blocks

    head = starts[1]
    arrived_0 = over_y(columns(1 - y, 0, head))
    scaled, frame_part, _ = gate_and_products(
        grad_out, branch_out, mod_gate, level_table, after(frame_ids, arrived_0), levels
    )
    order = [z, z ^ 1, jnp.where(is_mid, z ^ 3, z ^ 2), jnp.where(is_mid, z ^ 2, z ^ 3)]
    piece = scaled.shape[0]
    scaled = jnp.concatenate(
        [lax.dynamic_slice(scaled, (0, owner * block), (piece, block)) for owner in order], axis=1
    )
    def to_near(own):
        return along_z(own, [(0, 1), (1, 0), (2, 3), (3, 2)])

    def across(block):
        return along_z(block, [(1, 2), (2, 1)])

    def outward(block):
        return along_z(block, [(1, 0), (2, 3)])

    kept, received = [], []

    def multiply(pair, crossed, forwarded):
        far = jnp.where(is_mid, crossed, forwarded)
        full = jnp.concatenate([pair, far], axis=0)
        part = jnp.dot(other, full, preferred_element_type=jnp.float32).astype(jnp.bfloat16)
        received.append(over_y(part))
        kept.append(jnp.dot(mine, full, preferred_element_type=jnp.float32).astype(jnp.bfloat16))
        return part, kept[-1]

    own_0 = own_block(0, arrived_0, 0)
    near_0 = to_near(own_0)
    rest = over_y(after(columns(1 - y, head, half - head), arrived_0))

    gate = (near_0, rest)
    pairs = pairs_of(0, own_0, near_0)
    own_1 = own_block(1, rest, 0)
    near_1 = to_near(after(own_1, *gate))
    crossed_0 = across(after(pairs[0][1], *gate))
    mine_x = over_seq(after(scaled, *gate), 2)
    theirs = over_y(after(scaled, *gate))
    frame_part = seq_step(frame_part, seq, 2, gate)

    gate = (near_1, crossed_0, mine_x, theirs, frame_part)
    pairs += pairs_of(1, own_1, near_1)
    forwarded_0 = outward(after(crossed_0, *gate))
    crossed_1 = across(after(pairs[1][1], *gate))
    theirs_x = over_seq(after(theirs, *gate), 2)
    mine_core = over_seq(after(jnp.stack([scaled, mine_x]), *gate), 1)
    frame_grad = seq_step(frame_part, seq, 1, gate)
    packed = pack_frames(frame_grad, levels)

    gate = (forwarded_0, crossed_1, theirs_x, mine_core, packed)
    forwarded_1 = outward(after(crossed_1, *gate))
    crossed_2 = across(after(pairs[2][1], *gate))
    other_core = over_seq(after(jnp.stack([theirs, theirs_x]), *gate), 1)
    mine = order_pieces(me, [scaled, mine_core[0], mine_x, mine_core[1]])
    packed = clip_step(packed, dp, 1, gate)

    gate = (forwarded_1, crossed_2, mine, other_core, packed)
    forwarded_2 = outward(after(crossed_2, *gate))
    crossed_3 = across(after(pairs[3][1], *gate))
    packed = clip_step(packed, dp, 2, gate)
    other = order_pieces(me, [theirs, other_core[0], theirs_x, other_core[1]])
    products = multiply(after(pairs[0][1], packed), crossed_0, forwarded_0)
    products += multiply(after(pairs[1][1], packed), crossed_1, forwarded_1)

    gate = (forwarded_2, crossed_3, packed, *products)
    forwarded_3 = outward(after(crossed_3, *gate))
    packed = clip_step(packed, dp, 4, gate)
    table_grad = table_of(packed, level_table.shape[0])
    multiply(pairs[2][1], crossed_2, forwarded_2)
    multiply(pairs[3][1], crossed_3, forwarded_3)
    hidden_grad = assemble(y, [start for start, _ in pairs], kept, received)
    return hidden_grad[None], frame_grad[None], table_grad


def solution(mesh):
    staged = mesh.shape["dp"] == 8 and mesh.shape["seq"] == 4
    return jax.shard_map(
        staged_body if staged else plain_body,
        mesh=mesh,
        in_specs=(
            P("dp", "seq", None),
            P("dp", "seq", None),
            P("seq", "dp"),
            P(),
            P(),
            P("dp", "seq"),
            P("dp", None),
        ),
        out_specs=(P("dp", None, "seq"), P("dp", None, "seq"), P("dp", "seq")),
        check_vma=False,
    )
```

```python
import jax
import jax.numpy as jnp
from jax import lax
from jax.experimental import pallas as pl
from jax.experimental.pallas import tpu as pltpu
from jax.sharding import PartitionSpec as P

HIGHEST = lax.Precision.HIGHEST
CHUNKS = 4
BLOCKS = 2


def onehot(values, count):
    return (values[:, None] == jnp.arange(count, dtype=jnp.int32)[None, :]).astype(jnp.float32)


def gated(grad_out, mod_gate, level_table, frame_ids, levels):
    marks = onehot(levels[0], level_table.shape[0])
    gate_frames = mod_gate[None, :] + jnp.dot(marks, level_table, precision=HIGHEST)
    frames = onehot(frame_ids[0], levels.shape[1])
    gate_tokens = jnp.dot(frames, gate_frames, precision=HIGHEST)
    return (gate_tokens * grad_out[0].astype(jnp.float32)).astype(jnp.bfloat16)


def frame_sums(grad_out, branch_out, frame_ids, levels):
    products = grad_out[0].astype(jnp.float32) * branch_out[0].astype(jnp.float32)
    return jnp.dot(onehot(frame_ids[0], levels.shape[1]).T, products, precision=HIGHEST)


def plain_body(grad_out, branch_out, down_weight, mod_gate, level_table, frame_ids, levels):
    scaled = gated(grad_out, mod_gate, level_table, frame_ids, levels)
    frame_part = frame_sums(grad_out, branch_out, frame_ids, levels)
    hidden_grad = lax.dot_general(
        lax.all_gather(scaled, "seq", axis=0, tiled=True),
        lax.all_gather(down_weight, "dp", axis=1, tiled=True),
        (((1,), (1,)), ((), ())),
        preferred_element_type=jnp.float32,
    ).astype(jnp.bfloat16)
    frame_grad = lax.psum_scatter(frame_part, "seq", scatter_dimension=1, tiled=True)
    marks = onehot(levels[0], level_table.shape[0])
    level_part = jnp.dot(marks.T, frame_grad, precision=HIGHEST)
    table_grad = lax.psum_scatter(level_part, "dp", scatter_dimension=0, tiled=True)
    return hidden_grad[None], frame_grad[None], table_grad


def split_terms(values):
    terms = []
    for _ in range(3):
        term = lax.reduce_precision(values, exponent_bits=8, mantissa_bits=7)
        terms.append(term.astype(jnp.bfloat16))
        values = values - term
    return terms


def with_frame_lines(tokens, frame_part, levels, seq):
    frame_count, width = frame_part.shape
    level_line = jnp.pad(levels.astype(jnp.bfloat16), ((0, 0), (0, width // seq - frame_count)))
    level_line = jnp.tile(level_line, (1, seq))
    lines = jnp.concatenate([*split_terms(frame_part), level_line], axis=0)
    lines = jnp.pad(lines, ((0, -lines.shape[0] % 16), (0, 0)))
    return jnp.concatenate([tokens, lines], axis=0)


def frames_of(me, rows, frame_count, width, pieces):
    lines = pieces[0][0].shape[0] - rows
    any_space = pl.BlockSpec(memory_space=pl.ANY)

    def kernel(place, *refs):
        result, held, sems = refs[8], refs[9], refs[10]
        below = pl.ds(rows, lines)
        columns = pl.ds(pl.multiple_of(place[0] * width, 128), width)
        copies = []
        for ref, (_, index) in zip(refs, pieces):
            source = ref if index is None else ref.at[index]
            copies.append(
                pltpu.make_async_copy(
                    source.at[below, columns], held.at[len(copies)], sems.at[len(copies)]
                )
            )
            copies[-1].start()
        for copy in copies:
            copy.wait()
        for clip in range(2):
            total = jnp.zeros((lines, width), jnp.float32)
            for index in range(4):
                total = total + held[4 * clip + index].astype(jnp.float32)
            sums = total[:frame_count]
            for term in (1, 2):
                sums = sums + total[term * frame_count : (term + 1) * frame_count]
            result[clip, :frame_count] = sums
            marks = held[4 * clip].astype(jnp.float32)
            result[clip, frame_count:] = marks[3 * frame_count : 3 * frame_count + 1]

    return pl.pallas_call(
        kernel,
        out_shape=jax.ShapeDtypeStruct((2, frame_count + 1, width), jnp.float32),
        in_specs=[pl.BlockSpec(memory_space=pltpu.SMEM)] + [any_space] * 8,
        out_specs=pl.BlockSpec(memory_space=pltpu.VMEM),
        scratch_shapes=[
            pltpu.VMEM((8, lines, width), jnp.bfloat16),
            pltpu.SemaphoreType.DMA((8,)),
        ],
        name="frame_lines",
    )(me.astype(jnp.int32).reshape(1), *[array for array, _ in pieces])


def clip_step(packed, dp, flip, gate):
    sent = after(packed, *gate)
    arrived = lax.ppermute(sent, "dp", [(i, i ^ flip) for i in range(dp)])
    return jnp.concatenate([packed, arrived], axis=0)


def table_of(packed, level_count):
    dp, lines, width = packed.shape
    frame_count = lines - 1
    owned = level_count // dp
    rows = (lax.axis_index("dp") * owned + jnp.arange(owned, dtype=jnp.int32)).astype(jnp.float32)
    sums = packed[:, :frame_count].reshape(dp * frame_count, width)
    marks = packed[:, frame_count, :frame_count].reshape(dp * frame_count)
    owners = (rows[:, None] == marks[None, :]).astype(jnp.float32)
    return jnp.dot(owners, sums, precision=HIGHEST)


def after(array, *earlier):
    return lax.optimization_barrier((array, *earlier))[0]


def slice_rows(upper, lower, count):
    rows, columns = upper.shape
    width = columns // count
    vmem = pl.BlockSpec(memory_space=pltpu.VMEM)

    def kernel(upper, lower, *results):
        for index, result in enumerate(results):
            chunk = pl.ds(index * width, width)
            result[:rows] = upper[:, chunk]
            result[rows:] = lower[:, chunk]

    return pl.pallas_call(
        kernel,
        out_shape=[jax.ShapeDtypeStruct((2 * rows, width), upper.dtype)] * count,
        in_specs=[vmem, vmem],
        out_specs=[vmem] * count,
        compiler_params=pltpu.CompilerParams(vmem_limit_bytes=16 << 20),
        name="slice_rows",
    )(upper, lower)


def gather_rows(y, is_mid, start, width, own, near, crossed, forwarded, last, offset):
    rows = own[0].shape[0]
    vmem = pl.BlockSpec(memory_space=pltpu.VMEM)
    parts = [*own, *near, *crossed[0], *crossed[1], *forwarded]

    def kernel(place, *refs):
        result = refs[len(parts) + 1]
        first = pl.multiple_of(place[0] * rows, 16)
        second = pl.multiple_of((1 - place[0]) * rows, 16)
        chunk = pl.ds(start, width)

        def put(block, index):
            base = 2 * rows * block
            result[pl.ds(pl.multiple_of(base + first, 16), rows), :] = refs[index][:, chunk]
            result[pl.ds(pl.multiple_of(base + second, 16), rows), :] = refs[index + 1][:, chunk]

        put(0, 0)
        put(1, 2)

        @pl.when(place[1] == 1)
        def _():
            put(2, 4)
            put(3, 6)

        @pl.when(place[1] == 0)
        def _():
            put(2, 8)
            final = refs[len(parts)]
            inner = pl.ds(offset, width)
            base = 6 * rows
            result[pl.ds(pl.multiple_of(base + first, 16), rows), :] = final[:rows, inner]
            result[pl.ds(pl.multiple_of(base + second, 16), rows), :] = final[rows:, inner]

    return pl.pallas_call(
        kernel,
        out_shape=jax.ShapeDtypeStruct((8 * rows, width), last.dtype),
        in_specs=[pl.BlockSpec(memory_space=pltpu.SMEM)] + [vmem] * (len(parts) + 1),
        out_specs=vmem,
        compiler_params=pltpu.CompilerParams(vmem_limit_bytes=24 << 20),
        name="gather_rows",
    )(jnp.stack([y, is_mid.astype(jnp.int32)]).astype(jnp.int32), *parts, last)


def order_pieces(me, rows, pieces):
    count, width = 4, pieces[0][0].shape[1]
    any_space = pl.BlockSpec(memory_space=pl.ANY)

    def kernel(place, *refs):
        result, sems = refs[count], refs[count + 1]
        sources = [
            ref if index is None else ref.at[index] for ref, (_, index) in zip(refs, pieces)
        ]
        copies = []
        for flip in range(count):
            start = pl.multiple_of((place[0] ^ flip) * rows, 128)
            source = sources[flip].at[pl.ds(0, rows)]
            copies.append(
                pltpu.make_async_copy(source, result.at[pl.ds(start, rows)], sems.at[flip])
            )
            copies[-1].start()
        for copy in copies:
            copy.wait()

    return pl.pallas_call(
        kernel,
        out_shape=jax.ShapeDtypeStruct((count * rows, width), pieces[0][0].dtype),
        in_specs=[pl.BlockSpec(memory_space=pltpu.SMEM)] + [any_space] * count,
        out_specs=pl.BlockSpec(memory_space=pltpu.VMEM),
        scratch_shapes=[pltpu.SemaphoreType.DMA((count,))],
        compiler_params=pltpu.CompilerParams(vmem_limit_bytes=16 << 20),
        name="order_pieces",
    )(me.astype(jnp.int32).reshape(1), *[array for array, _ in pieces])


def place_columns(y, half, starts, kept, received, earlier=None):
    count, rows = len(kept), kept[0].shape[0]
    vmem = pl.BlockSpec(memory_space=pltpu.VMEM)
    any_space = pl.BlockSpec(memory_space=pl.ANY)
    held = [] if earlier is None else [earlier]

    def kernel(place, *refs):
        result, sems = refs[2 * count + len(held)], refs[2 * count + len(held) + 1]
        copies = []
        for index, start in enumerate(starts):
            for side, first in ((0, place[0] * half), (1, (1 - place[0]) * half)):
                source = refs[side * count + index]
                column = pl.multiple_of(first + start, 128)
                target = result.at[:, pl.ds(column, source.shape[1])]
                copies.append(
                    pltpu.make_async_copy(source, target, sems.at[2 * index + side])
                )
                copies[-1].start()
        for copy in copies:
            copy.wait()

    return pl.pallas_call(
        kernel,
        out_shape=jax.ShapeDtypeStruct((rows, 2 * half), kept[0].dtype),
        in_specs=[pl.BlockSpec(memory_space=pltpu.SMEM)]
        + [vmem] * (2 * count)
        + [any_space] * len(held),
        out_specs=any_space,
        input_output_aliases={2 * count + 1: 0} if held else {},
        scratch_shapes=[pltpu.SemaphoreType.DMA((2 * count,))],
        compiler_params=pltpu.CompilerParams(vmem_limit_bytes=16 << 20),
        name="place_columns",
    )(y.astype(jnp.int32).reshape(1), *kept, *received, *held)


def staged_body(grad_out, branch_out, down_weight, mod_gate, level_table, frame_ids, levels):
    dp, seq = 8, 4
    clip, me = lax.axis_index("dp"), lax.axis_index("seq")
    z, y = clip // 2, clip % 2
    is_mid = jnp.logical_or(z == 1, z == 2)
    hidden, shard = down_weight.shape
    half = hidden // 2
    block = 2 * shard

    def along_z(array, pairs):
        perm = [(a * 2 + s, b * 2 + s) for a, b in pairs for s in range(2)]
        return lax.ppermute(array, "dp", perm)

    def over_y(array):
        return lax.ppermute(array, "dp", [(i, i ^ 1) for i in range(dp)])

    def over_seq(array, flip):
        return lax.ppermute(array, "seq", [(i, i ^ flip) for i in range(seq)])

    def ordered(flag, first, second, axis):
        swapped = jnp.concatenate([second, first], axis=axis)
        return jnp.where(flag, swapped, jnp.concatenate([first, second], axis=axis))

    weight = down_weight.T
    width = half // CHUNKS
    own_p = lax.dynamic_slice(weight, (0, y * half), (shard, half))
    sent = lax.dynamic_slice(weight, (0, (1 - y) * half), (shard, half))

    scaled = gated(grad_out, mod_gate, level_table, frame_ids, levels)
    frame_part = frame_sums(grad_out, branch_out, frame_ids, levels)
    order = [z, z ^ 1, jnp.where(is_mid, z ^ 3, z ^ 2), jnp.where(is_mid, z ^ 2, z ^ 3)]
    piece = scaled.shape[0]
    scaled = jnp.concatenate(
        [lax.dynamic_slice(scaled, (0, owner * block), (piece, block)) for owner in order], axis=1
    )
    tokens = with_frame_lines(scaled, frame_part, levels, seq)
    def to_near(own):
        return along_z(own, [(0, 1), (1, 0), (2, 3), (3, 2)])

    def across(block):
        return along_z(block, [(1, 2), (2, 1)])

    def outward(block):
        return along_z(block, [(1, 0), (2, 3)])

    own_q = over_y(sent)
    near_p = to_near(own_p)
    crossed_p = across(own_p)

    gate = (own_q, near_p, crossed_p)
    mine_x = over_seq(after(tokens, *gate), 2)
    theirs = over_y(after(tokens, *gate))
    near_q = to_near(after(own_q, *gate))
    crossed_q = across(after(own_q, *gate))
    crossed_near_p = across(after(near_p, *gate))
    forwarded_p = outward(after(crossed_p, *gate, mine_x))

    gate = (near_q, crossed_q, crossed_near_p, forwarded_p)
    theirs_x = over_seq(after(theirs, *gate), 2)
    three_core = over_seq(after(jnp.stack([tokens, mine_x, theirs]), *gate), 1)
    crossed_near_q = across(after(near_q, *gate))
    forwarded_q = outward(after(crossed_q, *gate))

    gate = (crossed_near_q, forwarded_q, three_core, theirs_x)
    theirs_x_core = over_seq(after(theirs_x, *gate), 1)
    clips = (
        ((tokens, None), (three_core, 0), (mine_x, None), (three_core, 1)),
        ((theirs, None), (three_core, 2), (theirs_x, None), (theirs_x_core, None)),
    )
    mine, other = order_pieces(me, piece, clips[0]), order_pieces(me, piece, clips[1])
    frame_count = levels.shape[1]
    columns = shard * dp // seq
    packed = frames_of(me, piece, frame_count, columns, clips[0] + clips[1])
    frame_grad = packed[0, :frame_count]

    blocks = slice_rows(after(crossed_near_p, *gate), after(crossed_near_q, *gate), BLOCKS)
    last = [outward(block) for block in blocks]
    each = CHUNKS // BLOCKS
    kept, received, products = [], [], []
    firsts = [position * width for position in range(CHUNKS)]
    packed = clip_step(packed, dp, 2, (theirs_x_core,))
    packed = clip_step(packed, dp, 4, (last[0],))
    for index in range(CHUNKS):
        block, offset = last[index // each], index % each * width
        own = after(own_p, *products[: 2 * each]) if index >= each else own_p
        full = gather_rows(
            y,
            is_mid,
            index * width,
            width,
            (own, own_q),
            (near_p, near_q),
            ((crossed_p, crossed_q), (crossed_near_p, crossed_near_q)),
            (forwarded_p, forwarded_q),
            block,
            offset,
        )
        if index == CHUNKS - 1:
            result = place_columns(y, half, firsts[:2], kept[:2], received[:2])
            table_grad = table_of(packed, level_table.shape[0])
            full = after(full, result, table_grad)
        part = jnp.dot(other, full, preferred_element_type=jnp.float32).astype(jnp.bfloat16)
        received.append(over_y(part))
        kept.append(jnp.dot(mine, full, preferred_element_type=jnp.float32).astype(jnp.bfloat16))
        products += [part, kept[-1]]
    hidden_grad = place_columns(y, half, firsts[2:], kept[2:], received[2:], result)
    return hidden_grad[None], frame_grad[None], table_grad


def solution(mesh):
    staged = mesh.shape["dp"] == 8 and mesh.shape["seq"] == 4
    return jax.shard_map(
        staged_body if staged else plain_body,
        mesh=mesh,
        in_specs=(
            P("dp", "seq", None),
            P("dp", "seq", None),
            P("seq", "dp"),
            P(),
            P(),
            P("dp", "seq"),
            P("dp", None),
        ),
        out_specs=(P("dp", None, "seq"), P("dp", None, "seq"), P("dp", "seq")),
        check_vma=False,
    )
```

```python
import jax
import jax.numpy as jnp
from jax import lax
from jax.experimental import pallas as pl
from jax.experimental.pallas import tpu as pltpu
from jax.sharding import PartitionSpec as P

HIGHEST = lax.Precision.HIGHEST
CHUNKS = 4
BLOCKS = (2, 1, 1)


def onehot(values, count):
    return (values[:, None] == jnp.arange(count, dtype=jnp.int32)[None, :]).astype(jnp.float32)


def gated(grad_out, mod_gate, level_table, frame_ids, levels):
    marks = onehot(levels[0], level_table.shape[0])
    gate_frames = mod_gate[None, :] + jnp.dot(marks, level_table, precision=HIGHEST)
    frames = onehot(frame_ids[0], levels.shape[1])
    gate_tokens = jnp.dot(frames, gate_frames, precision=HIGHEST)
    return (gate_tokens * grad_out[0].astype(jnp.float32)).astype(jnp.bfloat16)


def frame_sums(grad_out, branch_out, frame_ids, levels):
    products = grad_out[0].astype(jnp.float32) * branch_out[0].astype(jnp.float32)
    return jnp.dot(onehot(frame_ids[0], levels.shape[1]).T, products, precision=HIGHEST)


def plain_body(grad_out, branch_out, down_weight, mod_gate, level_table, frame_ids, levels):
    scaled = gated(grad_out, mod_gate, level_table, frame_ids, levels)
    frame_part = frame_sums(grad_out, branch_out, frame_ids, levels)
    hidden_grad = lax.dot_general(
        lax.all_gather(scaled, "seq", axis=0, tiled=True),
        lax.all_gather(down_weight, "dp", axis=1, tiled=True),
        (((1,), (1,)), ((), ())),
        preferred_element_type=jnp.float32,
    ).astype(jnp.bfloat16)
    frame_grad = lax.psum_scatter(frame_part, "seq", scatter_dimension=1, tiled=True)
    marks = onehot(levels[0], level_table.shape[0])
    level_part = jnp.dot(marks.T, frame_grad, precision=HIGHEST)
    table_grad = lax.psum_scatter(level_part, "dp", scatter_dimension=0, tiled=True)
    return hidden_grad[None], frame_grad[None], table_grad


def split_terms(values):
    terms = []
    for _ in range(3):
        term = lax.reduce_precision(values, exponent_bits=8, mantissa_bits=7)
        terms.append(term.astype(jnp.bfloat16))
        values = values - term
    return terms


def with_frame_lines(tokens, frame_part, levels, seq):
    frame_count, width = frame_part.shape
    level_line = jnp.pad(levels.astype(jnp.bfloat16), ((0, 0), (0, width // seq - frame_count)))
    level_line = jnp.tile(level_line, (1, seq))
    lines = jnp.concatenate([*split_terms(frame_part), level_line], axis=0)
    lines = jnp.pad(lines, ((0, -lines.shape[0] % 16), (0, 0)))
    return jnp.concatenate([tokens, lines], axis=0)


def frames_of(me, rows, frame_count, width, pieces):
    lines = pieces[0][0].shape[0] - rows
    any_space = pl.BlockSpec(memory_space=pl.ANY)

    def kernel(place, *refs):
        result, held, sems = refs[8], refs[9], refs[10]
        below = pl.ds(rows, lines)
        columns = pl.ds(pl.multiple_of(place[0] * width, 128), width)
        copies = []
        for ref, (_, index) in zip(refs, pieces):
            source = ref if index is None else ref.at[index]
            copies.append(
                pltpu.make_async_copy(
                    source.at[below, columns], held.at[len(copies)], sems.at[len(copies)]
                )
            )
            copies[-1].start()
        for copy in copies:
            copy.wait()
        for clip in range(2):
            total = jnp.zeros((lines, width), jnp.float32)
            for index in range(4):
                total = total + held[4 * clip + index].astype(jnp.float32)
            sums = total[:frame_count]
            for term in (1, 2):
                sums = sums + total[term * frame_count : (term + 1) * frame_count]
            result[clip, :frame_count] = sums
            marks = held[4 * clip].astype(jnp.float32)
            result[clip, frame_count:] = marks[3 * frame_count : 3 * frame_count + 1]

    return pl.pallas_call(
        kernel,
        out_shape=jax.ShapeDtypeStruct((2, frame_count + 1, width), jnp.float32),
        in_specs=[pl.BlockSpec(memory_space=pltpu.SMEM)] + [any_space] * 8,
        out_specs=pl.BlockSpec(memory_space=pltpu.VMEM),
        scratch_shapes=[
            pltpu.VMEM((8, lines, width), jnp.bfloat16),
            pltpu.SemaphoreType.DMA((8,)),
        ],
        name="frame_lines",
    )(me.astype(jnp.int32).reshape(1), *[array for array, _ in pieces])


def clip_step(packed, dp, flip, gate):
    sent = after(packed, *gate)
    arrived = lax.ppermute(sent, "dp", [(i, i ^ flip) for i in range(dp)])
    return jnp.concatenate([packed, arrived], axis=0)


def table_of(packed, level_count):
    dp, lines, width = packed.shape
    frame_count = lines - 1
    owned = level_count // dp
    rows = (lax.axis_index("dp") * owned + jnp.arange(owned, dtype=jnp.int32)).astype(jnp.float32)
    sums = packed[:, :frame_count].reshape(dp * frame_count, width)
    marks = packed[:, frame_count, :frame_count].reshape(dp * frame_count)
    owners = (rows[:, None] == marks[None, :]).astype(jnp.float32)
    return jnp.dot(owners, sums, precision=HIGHEST)


def after(array, *earlier):
    return lax.optimization_barrier((array, *earlier))[0]


def slice_rows(upper, lower, widths):
    rows = upper.shape[0]
    vmem = pl.BlockSpec(memory_space=pltpu.VMEM)

    def kernel(upper, lower, *results):
        for index, result in enumerate(results):
            chunk = pl.ds(sum(widths[:index]), widths[index])
            result[:rows] = upper[:, chunk]
            result[rows:] = lower[:, chunk]

    return pl.pallas_call(
        kernel,
        out_shape=[jax.ShapeDtypeStruct((2 * rows, width), upper.dtype) for width in widths],
        in_specs=[vmem, vmem],
        out_specs=[vmem] * len(widths),
        compiler_params=pltpu.CompilerParams(vmem_limit_bytes=16 << 20),
        name="slice_rows",
    )(upper, lower)


def block_rows(y, is_mid, blocks):
    rows, width = blocks[0][0].shape
    vmem = pl.BlockSpec(memory_space=pltpu.VMEM)
    parts = [part for block in blocks for part in block]

    def kernel(place, *refs):
        result = refs[len(parts)]
        first = pl.multiple_of(place[0] * rows, 16)
        second = pl.multiple_of((1 - place[0]) * rows, 16)

        def put(block, upper, lower):
            base = 2 * rows * block
            result[pl.ds(pl.multiple_of(base + first, 16), rows), :] = upper[...]
            result[pl.ds(pl.multiple_of(base + second, 16), rows), :] = lower[...]

        index = 0
        for position, block in enumerate(blocks):
            held = refs[index : index + len(block)]
            index += len(block)
            if len(block) == 2:
                put(position, *held)
            else:
                pl.when(place[1] == 1)(lambda: put(position, *held[:2]))
                pl.when(place[1] == 0)(lambda: put(position, *held[2:]))

    return pl.pallas_call(
        kernel,
        out_shape=jax.ShapeDtypeStruct((2 * rows * len(blocks), width), parts[0].dtype),
        in_specs=[pl.BlockSpec(memory_space=pltpu.SMEM)] + [vmem] * len(parts),
        out_specs=vmem,
        compiler_params=pltpu.CompilerParams(vmem_limit_bytes=24 << 20),
        name="block_rows",
    )(jnp.stack([y, is_mid.astype(jnp.int32)]).astype(jnp.int32), *parts)


def last_rows(y, is_mid, width, sent, arrived, offset):
    rows = sent.shape[0] // 2
    vmem = pl.BlockSpec(memory_space=pltpu.VMEM)

    def kernel(place, sent, arrived, result):
        def put(source):
            first = pl.ds(pl.multiple_of(place[0] * rows, 16), rows)
            second = pl.ds(pl.multiple_of((1 - place[0]) * rows, 16), rows)
            result[first, :] = source[:rows, offset : offset + width]
            result[second, :] = source[rows:, offset : offset + width]

        pl.when(place[1] == 1)(lambda: put(sent))
        pl.when(place[1] == 0)(lambda: put(arrived))

    return pl.pallas_call(
        kernel,
        out_shape=jax.ShapeDtypeStruct((2 * rows, width), sent.dtype),
        in_specs=[pl.BlockSpec(memory_space=pltpu.SMEM)] + [vmem] * 2,
        out_specs=vmem,
        compiler_params=pltpu.CompilerParams(vmem_limit_bytes=16 << 20),
        name="last_rows",
    )(jnp.stack([y, is_mid.astype(jnp.int32)]).astype(jnp.int32), sent, arrived)


def order_pieces(me, rows, widths, pieces):
    count, groups = 4, len(widths)
    any_space = pl.BlockSpec(memory_space=pl.ANY)

    def kernel(place, *refs):
        results, sems = refs[count : count + groups], refs[count + groups]
        sources = [
            ref if index is None else ref.at[index] for ref, (_, index) in zip(refs, pieces)
        ]
        copies = []
        for side, width in enumerate(widths):
            columns = pl.ds(sum(widths[:side]), width)
            for flip in range(count):
                start = pl.multiple_of((place[0] ^ flip) * rows, 128)
                source = sources[flip].at[pl.ds(0, rows), columns]
                target = results[side].at[pl.ds(start, rows)]
                copies.append(pltpu.make_async_copy(source, target, sems.at[side * count + flip]))
                copies[-1].start()
        for copy in copies:
            copy.wait()

    return pl.pallas_call(
        kernel,
        out_shape=[
            jax.ShapeDtypeStruct((count * rows, width), pieces[0][0].dtype) for width in widths
        ],
        in_specs=[pl.BlockSpec(memory_space=pltpu.SMEM)] + [any_space] * count,
        out_specs=[pl.BlockSpec(memory_space=pltpu.VMEM)] * groups,
        scratch_shapes=[pltpu.SemaphoreType.DMA((groups * count,))],
        compiler_params=pltpu.CompilerParams(vmem_limit_bytes=16 << 20),
        name="order_pieces",
    )(me.astype(jnp.int32).reshape(1), *[array for array, _ in pieces])


def place_columns(y, half, starts, kept, received, earlier=None):
    count, rows = len(kept), kept[0].shape[0]
    vmem = pl.BlockSpec(memory_space=pltpu.VMEM)
    any_space = pl.BlockSpec(memory_space=pl.ANY)
    held = [] if earlier is None else [earlier]

    def kernel(place, *refs):
        result, sems = refs[2 * count + len(held)], refs[2 * count + len(held) + 1]
        copies = []
        for index, start in enumerate(starts):
            for side, first in ((0, place[0] * half), (1, (1 - place[0]) * half)):
                source = refs[side * count + index]
                column = pl.multiple_of(first + start, 128)
                target = result.at[:, pl.ds(column, source.shape[1])]
                copies.append(
                    pltpu.make_async_copy(source, target, sems.at[2 * index + side])
                )
                copies[-1].start()
        for copy in copies:
            copy.wait()

    return pl.pallas_call(
        kernel,
        out_shape=jax.ShapeDtypeStruct((rows, 2 * half), kept[0].dtype),
        in_specs=[pl.BlockSpec(memory_space=pltpu.SMEM)]
        + [vmem] * (2 * count)
        + [any_space] * len(held),
        out_specs=any_space,
        input_output_aliases={2 * count + 1: 0} if held else {},
        scratch_shapes=[pltpu.SemaphoreType.DMA((2 * count,))],
        compiler_params=pltpu.CompilerParams(vmem_limit_bytes=16 << 20),
        name="place_columns",
    )(y.astype(jnp.int32).reshape(1), *kept, *received, *held)


def staged_body(grad_out, branch_out, down_weight, mod_gate, level_table, frame_ids, levels):
    dp, seq = 8, 4
    clip, me = lax.axis_index("dp"), lax.axis_index("seq")
    z, y = clip // 2, clip % 2
    is_mid = jnp.logical_or(z == 1, z == 2)
    hidden, shard = down_weight.shape
    half = hidden // 2
    block = 2 * shard

    def along_z(array, pairs):
        perm = [(a * 2 + s, b * 2 + s) for a, b in pairs for s in range(2)]
        return lax.ppermute(array, "dp", perm)

    def over_y(array):
        return lax.ppermute(array, "dp", [(i, i ^ 1) for i in range(dp)])

    def over_seq(array, flip):
        return lax.ppermute(array, "seq", [(i, i ^ flip) for i in range(seq)])

    def ordered(flag, first, second, axis):
        swapped = jnp.concatenate([second, first], axis=axis)
        return jnp.where(flag, swapped, jnp.concatenate([first, second], axis=axis))

    weight = down_weight.T
    width = half // CHUNKS
    own_p = lax.dynamic_slice(weight, (0, y * half), (shard, half))
    sent = lax.dynamic_slice(weight, (0, (1 - y) * half), (shard, half))

    scaled = gated(grad_out, mod_gate, level_table, frame_ids, levels)
    frame_part = frame_sums(grad_out, branch_out, frame_ids, levels)
    order = [z, z ^ 1, jnp.where(is_mid, z ^ 3, z ^ 2), jnp.where(is_mid, z ^ 2, z ^ 3)]
    piece = scaled.shape[0]
    scaled = jnp.concatenate(
        [lax.dynamic_slice(scaled, (0, owner * block), (piece, block)) for owner in order], axis=1
    )
    tokens = with_frame_lines(scaled, frame_part, levels, seq)
    def to_near(own):
        return along_z(own, [(0, 1), (1, 0), (2, 3), (3, 2)])

    def across(block):
        return along_z(block, [(1, 2), (2, 1)])

    def outward(block):
        return along_z(block, [(1, 0), (2, 3)])

    own_q = over_y(sent)
    near_p = to_near(own_p)
    crossed_p = across(own_p)

    gate = (own_q, near_p, crossed_p)
    mine_x = over_seq(after(tokens, *gate), 2)
    theirs = over_y(after(tokens, *gate))
    near_q = to_near(after(own_q, *gate))
    crossed_q = across(after(own_q, *gate))
    crossed_near_p = across(after(near_p, *gate))
    forwarded_p = outward(after(crossed_p, *gate, mine_x))

    gate = (near_q, crossed_q, crossed_near_p, forwarded_p)
    theirs_x = over_seq(after(theirs, *gate), 2)
    crossed_near_q = across(after(near_q, *gate))
    forwarded_q = outward(after(crossed_q, *gate))

    own_rows = block_rows(y, is_mid, ((own_p, own_q), (near_p, near_q)))

    gate = (crossed_near_q, forwarded_q, theirs_x)
    three_core = over_seq(after(jnp.stack([tokens, mine_x, theirs]), *gate, own_rows), 1)
    theirs_x_core = over_seq(after(theirs_x, *gate), 1)
    clips = (
        ((tokens, None), (three_core, 0), (mine_x, None), (three_core, 1)),
        ((theirs, None), (three_core, 2), (theirs_x, None), (theirs_x_core, None)),
    )
    cuts = (2 * block, block, block)
    mine = order_pieces(me, piece, cuts, clips[0])
    other = order_pieces(me, piece, cuts, clips[1])
    far = (after(crossed_p, three_core), crossed_q, forwarded_p, forwarded_q)
    far_rows = block_rows(y, is_mid, (far,))

    def first_sum(first, second):
        return jnp.dot(first, own_rows, preferred_element_type=jnp.float32) + jnp.dot(
            second, far_rows, preferred_element_type=jnp.float32
        )

    frame_count = levels.shape[1]
    columns = shard * dp // seq
    packed = frames_of(me, piece, frame_count, columns, clips[0] + clips[1])
    frame_grad = packed[0, :frame_count]
    other_sum = first_sum(other[0], other[1])
    mine_sum = first_sum(after(mine[0], packed), mine[1])

    blocks = slice_rows(
        after(crossed_near_p, *gate),
        after(crossed_near_q, *gate),
        [count * width for count in BLOCKS],
    )
    last = [outward(arrived) for arrived in blocks]
    places = [
        (sent, arrived, offset * width)
        for sent, arrived, count in zip(blocks, last, BLOCKS)
        for offset in range(count)
    ]
    firsts = [position * width for position in range(CHUNKS)]
    kept, received, parts, rows = [], [], [], []

    def finish(earlier, tokens_last, index):
        product = jnp.dot(tokens_last, rows[index], preferred_element_type=jnp.float32)
        return (earlier[:, firsts[index] : firsts[index] + width] + product).astype(jnp.bfloat16)

    for index, (sent, arrived, offset) in enumerate(places):
        if index < 2:
            sent = after(sent, other_sum, mine_sum)
        if index == 2:
            packed = clip_step(packed, dp, 2, (parts[1],))
            sent = after(sent, packed, *parts)
        if index == 3:
            packed = clip_step(packed, dp, 4, (parts[2],))
            sent = after(sent, packed, *kept)
        rows.append(last_rows(y, is_mid, width, sent, arrived, offset))
        parts.append(finish(other_sum, other[2], index))
        received.append(over_y(parts[index]))
        if index % 2:
            tokens_last = after(mine[2], parts[index])
            kept += [finish(mine_sum, tokens_last, done) for done in (index - 1, index)]
    table_grad = table_of(packed, level_table.shape[0])
    result = place_columns(after(y, parts[-1]), half, firsts[:2], kept[:2], received[:2])
    hidden_grad = place_columns(y, half, firsts[2:], kept[2:], received[2:], result)
    return hidden_grad[None], frame_grad[None], table_grad


def solution(mesh):
    staged = mesh.shape["dp"] == 8 and mesh.shape["seq"] == 4
    return jax.shard_map(
        staged_body if staged else plain_body,
        mesh=mesh,
        in_specs=(
            P("dp", "seq", None),
            P("dp", "seq", None),
            P("seq", "dp"),
            P(),
            P(),
            P("dp", "seq"),
            P("dp", None),
        ),
        out_specs=(P("dp", None, "seq"), P("dp", None, "seq"), P("dp", "seq")),
        check_vma=False,
    )
```

```python
import jax
import jax.numpy as jnp
from jax import lax
from jax.experimental import pallas as pl
from jax.experimental.pallas import tpu as pltpu
from jax.sharding import PartitionSpec as P

HIGHEST = lax.Precision.HIGHEST
CHUNKS = 4
BLOCKS = (2, 1, 1)


def onehot(values, count):
    return (values[:, None] == jnp.arange(count, dtype=jnp.int32)[None, :]).astype(jnp.float32)


def gated(grad_out, mod_gate, level_table, frame_ids, levels):
    marks = onehot(levels[0], level_table.shape[0])
    gate_frames = mod_gate[None, :] + jnp.dot(marks, level_table, precision=HIGHEST)
    frames = onehot(frame_ids[0], levels.shape[1])
    gate_tokens = jnp.dot(frames, gate_frames, precision=HIGHEST)
    return (gate_tokens * grad_out[0].astype(jnp.float32)).astype(jnp.bfloat16)


def frame_sums(grad_out, branch_out, frame_ids, levels):
    products = grad_out[0].astype(jnp.float32) * branch_out[0].astype(jnp.float32)
    return jnp.dot(onehot(frame_ids[0], levels.shape[1]).T, products, precision=HIGHEST)


def plain_body(grad_out, branch_out, down_weight, mod_gate, level_table, frame_ids, levels):
    scaled = gated(grad_out, mod_gate, level_table, frame_ids, levels)
    frame_part = frame_sums(grad_out, branch_out, frame_ids, levels)
    hidden_grad = lax.dot_general(
        lax.all_gather(scaled, "seq", axis=0, tiled=True),
        lax.all_gather(down_weight, "dp", axis=1, tiled=True),
        (((1,), (1,)), ((), ())),
        preferred_element_type=jnp.float32,
    ).astype(jnp.bfloat16)
    frame_grad = lax.psum_scatter(frame_part, "seq", scatter_dimension=1, tiled=True)
    marks = onehot(levels[0], level_table.shape[0])
    level_part = jnp.dot(marks.T, frame_grad, precision=HIGHEST)
    table_grad = lax.psum_scatter(level_part, "dp", scatter_dimension=0, tiled=True)
    return hidden_grad[None], frame_grad[None], table_grad


def split_terms(values):
    terms = []
    for _ in range(3):
        term = lax.reduce_precision(values, exponent_bits=8, mantissa_bits=7)
        terms.append(term.astype(jnp.bfloat16))
        values = values - term
    return terms


def with_frame_lines(tokens, frame_part, levels, seq):
    frame_count, width = frame_part.shape
    level_line = jnp.pad(levels.astype(jnp.bfloat16), ((0, 0), (0, width // seq - frame_count)))
    level_line = jnp.tile(level_line, (1, seq))
    lines = jnp.concatenate([*split_terms(frame_part), level_line], axis=0)
    lines = jnp.pad(lines, ((0, -lines.shape[0] % 16), (0, 0)))
    return jnp.concatenate([tokens, lines], axis=0)


def frames_of(me, rows, frame_count, width, pieces):
    lines = pieces[0][0].shape[0] - rows
    any_space = pl.BlockSpec(memory_space=pl.ANY)

    def kernel(place, *refs):
        result, held, sems = refs[8], refs[9], refs[10]
        below = pl.ds(rows, lines)
        columns = pl.ds(pl.multiple_of(place[0] * width, 128), width)
        copies = []
        for ref, (_, index) in zip(refs, pieces):
            source = ref if index is None else ref.at[index]
            copies.append(
                pltpu.make_async_copy(
                    source.at[below, columns], held.at[len(copies)], sems.at[len(copies)]
                )
            )
            copies[-1].start()
        for copy in copies:
            copy.wait()
        for clip in range(2):
            total = jnp.zeros((lines, width), jnp.float32)
            for index in range(4):
                total = total + held[4 * clip + index].astype(jnp.float32)
            sums = total[:frame_count]
            for term in (1, 2):
                sums = sums + total[term * frame_count : (term + 1) * frame_count]
            result[clip, :frame_count] = sums
            marks = held[4 * clip].astype(jnp.float32)
            result[clip, frame_count:] = marks[3 * frame_count : 3 * frame_count + 1]

    return pl.pallas_call(
        kernel,
        out_shape=jax.ShapeDtypeStruct((2, frame_count + 1, width), jnp.float32),
        in_specs=[pl.BlockSpec(memory_space=pltpu.SMEM)] + [any_space] * 8,
        out_specs=pl.BlockSpec(memory_space=pltpu.VMEM),
        scratch_shapes=[
            pltpu.VMEM((8, lines, width), jnp.bfloat16),
            pltpu.SemaphoreType.DMA((8,)),
        ],
        name="frame_lines",
    )(me.astype(jnp.int32).reshape(1), *[array for array, _ in pieces])


def clip_step(packed, dp, flip, gate):
    sent = after(packed, *gate)
    arrived = lax.ppermute(sent, "dp", [(i, i ^ flip) for i in range(dp)])
    return jnp.concatenate([packed, arrived], axis=0)


def table_of(packed, level_count):
    dp, lines, width = packed.shape
    frame_count = lines - 1
    owned = level_count // dp
    rows = (lax.axis_index("dp") * owned + jnp.arange(owned, dtype=jnp.int32)).astype(jnp.float32)
    sums = packed[:, :frame_count].reshape(dp * frame_count, width)
    marks = packed[:, frame_count, :frame_count].reshape(dp * frame_count)
    owners = (rows[:, None] == marks[None, :]).astype(jnp.float32)
    return jnp.dot(owners, sums, precision=HIGHEST)


def after(array, *earlier):
    return lax.optimization_barrier((array, *earlier))[0]


def slice_rows(upper, lower, widths):
    rows = upper.shape[0]
    vmem = pl.BlockSpec(memory_space=pltpu.VMEM)

    def kernel(upper, lower, *results):
        for index, result in enumerate(results):
            chunk = pl.ds(sum(widths[:index]), widths[index])
            result[:rows] = upper[:, chunk]
            result[rows:] = lower[:, chunk]

    return pl.pallas_call(
        kernel,
        out_shape=[jax.ShapeDtypeStruct((2 * rows, width), upper.dtype) for width in widths],
        in_specs=[vmem, vmem],
        out_specs=[vmem] * len(widths),
        compiler_params=pltpu.CompilerParams(vmem_limit_bytes=16 << 20),
        name="slice_rows",
    )(upper, lower)


def block_rows(y, is_mid, blocks):
    rows, width = blocks[0][0].shape
    vmem = pl.BlockSpec(memory_space=pltpu.VMEM)
    parts = [part for block in blocks for part in block]

    def kernel(place, *refs):
        result = refs[len(parts)]
        first = pl.multiple_of(place[0] * rows, 16)
        second = pl.multiple_of((1 - place[0]) * rows, 16)

        def put(block, upper, lower):
            base = 2 * rows * block
            result[pl.ds(pl.multiple_of(base + first, 16), rows), :] = upper[...]
            result[pl.ds(pl.multiple_of(base + second, 16), rows), :] = lower[...]

        index = 0
        for position, block in enumerate(blocks):
            held = refs[index : index + len(block)]
            index += len(block)
            if len(block) == 2:
                put(position, *held)
            else:
                pl.when(place[1] == 1)(lambda: put(position, *held[:2]))
                pl.when(place[1] == 0)(lambda: put(position, *held[2:]))

    return pl.pallas_call(
        kernel,
        out_shape=jax.ShapeDtypeStruct((2 * rows * len(blocks), width), parts[0].dtype),
        in_specs=[pl.BlockSpec(memory_space=pltpu.SMEM)] + [vmem] * len(parts),
        out_specs=vmem,
        compiler_params=pltpu.CompilerParams(vmem_limit_bytes=24 << 20),
        name="block_rows",
    )(jnp.stack([y, is_mid.astype(jnp.int32)]).astype(jnp.int32), *parts)


def last_rows(y, is_mid, width, sent, arrived, offset):
    rows = sent.shape[0] // 2
    vmem = pl.BlockSpec(memory_space=pltpu.VMEM)

    def kernel(place, sent, arrived, result):
        def put(source):
            first = pl.ds(pl.multiple_of(place[0] * rows, 16), rows)
            second = pl.ds(pl.multiple_of((1 - place[0]) * rows, 16), rows)
            result[first, :] = source[:rows, offset : offset + width]
            result[second, :] = source[rows:, offset : offset + width]

        pl.when(place[1] == 1)(lambda: put(sent))
        pl.when(place[1] == 0)(lambda: put(arrived))

    return pl.pallas_call(
        kernel,
        out_shape=jax.ShapeDtypeStruct((2 * rows, width), sent.dtype),
        in_specs=[pl.BlockSpec(memory_space=pltpu.SMEM)] + [vmem] * 2,
        out_specs=vmem,
        compiler_params=pltpu.CompilerParams(vmem_limit_bytes=16 << 20),
        name="last_rows",
    )(jnp.stack([y, is_mid.astype(jnp.int32)]).astype(jnp.int32), sent, arrived)


def order_pieces(me, rows, widths, pieces):
    count, groups = 4, len(widths)
    any_space = pl.BlockSpec(memory_space=pl.ANY)

    def kernel(place, *refs):
        results, sems = refs[count : count + groups], refs[count + groups]
        sources = [
            ref if index is None else ref.at[index] for ref, (_, index) in zip(refs, pieces)
        ]
        copies = []
        for side, width in enumerate(widths):
            columns = pl.ds(sum(widths[:side]), width)
            for flip in range(count):
                start = pl.multiple_of((place[0] ^ flip) * rows, 128)
                source = sources[flip].at[pl.ds(0, rows), columns]
                target = results[side].at[pl.ds(start, rows)]
                copies.append(pltpu.make_async_copy(source, target, sems.at[side * count + flip]))
                copies[-1].start()
        for copy in copies:
            copy.wait()

    return pl.pallas_call(
        kernel,
        out_shape=[
            jax.ShapeDtypeStruct((count * rows, width), pieces[0][0].dtype) for width in widths
        ],
        in_specs=[pl.BlockSpec(memory_space=pltpu.SMEM)] + [any_space] * count,
        out_specs=[pl.BlockSpec(memory_space=pltpu.VMEM)] * groups,
        scratch_shapes=[pltpu.SemaphoreType.DMA((groups * count,))],
        compiler_params=pltpu.CompilerParams(vmem_limit_bytes=16 << 20),
        name="order_pieces",
    )(me.astype(jnp.int32).reshape(1), *[array for array, _ in pieces])


def place_columns(y, half, starts, kept, received, earlier=None):
    count, rows = len(kept), kept[0].shape[0]
    vmem = pl.BlockSpec(memory_space=pltpu.VMEM)
    any_space = pl.BlockSpec(memory_space=pl.ANY)
    held = [] if earlier is None else [earlier]

    def kernel(place, *refs):
        result, sems = refs[2 * count + len(held)], refs[2 * count + len(held) + 1]
        copies = []
        for index, start in enumerate(starts):
            for side, first in ((0, place[0] * half), (1, (1 - place[0]) * half)):
                source = refs[side * count + index]
                column = pl.multiple_of(first + start, 128)
                target = result.at[:, pl.ds(column, source.shape[1])]
                copies.append(
                    pltpu.make_async_copy(source, target, sems.at[2 * index + side])
                )
                copies[-1].start()
        for copy in copies:
            copy.wait()

    return pl.pallas_call(
        kernel,
        out_shape=jax.ShapeDtypeStruct((rows, 2 * half), kept[0].dtype),
        in_specs=[pl.BlockSpec(memory_space=pltpu.SMEM)]
        + [vmem] * (2 * count)
        + [any_space] * len(held),
        out_specs=any_space,
        input_output_aliases={2 * count + 1: 0} if held else {},
        scratch_shapes=[pltpu.SemaphoreType.DMA((2 * count,))],
        compiler_params=pltpu.CompilerParams(vmem_limit_bytes=16 << 20),
        name="place_columns",
    )(y.astype(jnp.int32).reshape(1), *kept, *received, *held)


def staged_body(grad_out, branch_out, down_weight, mod_gate, level_table, frame_ids, levels):
    dp, seq = 8, 4
    clip, me = lax.axis_index("dp"), lax.axis_index("seq")
    z, y = clip // 2, clip % 2
    is_mid = jnp.logical_or(z == 1, z == 2)
    hidden, shard = down_weight.shape
    half = hidden // 2
    block = 2 * shard

    def along_z(array, pairs):
        perm = [(a * 2 + s, b * 2 + s) for a, b in pairs for s in range(2)]
        return lax.ppermute(array, "dp", perm)

    def over_y(array):
        return lax.ppermute(array, "dp", [(i, i ^ 1) for i in range(dp)])

    def over_seq(array, flip):
        return lax.ppermute(array, "seq", [(i, i ^ flip) for i in range(seq)])

    def ordered(flag, first, second, axis):
        swapped = jnp.concatenate([second, first], axis=axis)
        return jnp.where(flag, swapped, jnp.concatenate([first, second], axis=axis))

    weight = down_weight.T
    width = half // CHUNKS
    own_p = lax.dynamic_slice(weight, (0, y * half), (shard, half))
    sent = lax.dynamic_slice(weight, (0, (1 - y) * half), (shard, half))

    scaled = gated(grad_out, mod_gate, level_table, frame_ids, levels)
    frame_part = frame_sums(grad_out, branch_out, frame_ids, levels)
    order = [z, z ^ 1, jnp.where(is_mid, z ^ 3, z ^ 2), jnp.where(is_mid, z ^ 2, z ^ 3)]
    piece = scaled.shape[0]
    scaled = jnp.concatenate(
        [lax.dynamic_slice(scaled, (0, owner * block), (piece, block)) for owner in order], axis=1
    )
    tokens = with_frame_lines(scaled, frame_part, levels, seq)
    def to_near(own):
        return along_z(own, [(0, 1), (1, 0), (2, 3), (3, 2)])

    def across(block):
        return along_z(block, [(1, 2), (2, 1)])

    def outward(block):
        return along_z(block, [(1, 0), (2, 3)])

    own_q = over_y(sent)
    near_p = to_near(own_p)
    crossed_p = across(own_p)

    gate = (own_q, near_p, crossed_p)
    mine_x = over_seq(after(tokens, *gate), 2)
    theirs = over_y(after(tokens, *gate))
    near_q = to_near(after(own_q, *gate))
    crossed_q = across(after(own_q, *gate))
    crossed_near_p = across(after(near_p, *gate))
    forwarded_p = outward(after(crossed_p, *gate, mine_x))

    gate = (near_q, crossed_q, crossed_near_p, forwarded_p)
    theirs_x = over_seq(after(theirs, *gate), 2)
    crossed_near_q = across(after(near_q, *gate))
    forwarded_q = outward(after(crossed_q, *gate))

    own_rows = block_rows(y, is_mid, ((own_p, own_q), (near_p, near_q)))

    gate = (crossed_near_q, forwarded_q, theirs_x)
    three_core = over_seq(after(jnp.stack([tokens, mine_x, theirs]), *gate, own_rows), 1)
    theirs_x_core = over_seq(after(theirs_x, *gate), 1)
    clips = (
        ((tokens, None), (three_core, 0), (mine_x, None), (three_core, 1)),
        ((theirs, None), (three_core, 2), (theirs_x, None), (theirs_x_core, None)),
    )
    cuts = (2 * block, block, block)
    mine = order_pieces(me, piece, cuts, clips[0])
    other = order_pieces(me, piece, cuts, clips[1])
    far = (after(crossed_p, three_core), crossed_q, forwarded_p, forwarded_q)
    far_rows = block_rows(y, is_mid, (far,))

    def first_sum(first, second):
        return jnp.dot(first, own_rows, preferred_element_type=jnp.float32) + jnp.dot(
            second, far_rows, preferred_element_type=jnp.float32
        )

    frame_count = levels.shape[1]
    columns = shard * dp // seq
    packed = frames_of(me, piece, frame_count, columns, clips[0] + clips[1])
    frame_grad = packed[0, :frame_count]
    other_sum = first_sum(other[0], other[1])

    blocks = slice_rows(
        after(crossed_near_p, *gate),
        after(crossed_near_q, *gate),
        [count * width for count in BLOCKS],
    )
    last = [outward(arrived) for arrived in blocks]
    places = [
        (sent, arrived, offset * width)
        for sent, arrived, count in zip(blocks, last, BLOCKS)
        for offset in range(count)
    ]
    firsts = [position * width for position in range(CHUNKS)]
    received, parts, rows = [], [], []

    def finish(earlier, tokens_last, index):
        product = jnp.dot(tokens_last, rows[index], preferred_element_type=jnp.float32)
        return (earlier[:, firsts[index] : firsts[index] + width] + product).astype(jnp.bfloat16)

    for index, (sent, arrived, offset) in enumerate(places):
        if index < 2:
            sent = after(sent, other_sum)
        if index == 2:
            packed = clip_step(packed, dp, 2, (parts[1],))
            sent = after(sent, packed, *parts)
        if index == 3:
            packed = clip_step(packed, dp, 4, (parts[2],))
            sent = after(sent, packed, mine_sum)
        rows.append(last_rows(y, is_mid, width, sent, arrived, offset))
        parts.append(finish(other_sum, other[2], index))
        received.append(over_y(parts[index]))
        if index == 1:
            mine_sum = first_sum(after(mine[0], parts[1]), mine[1])
    tokens_last = after(mine[2], parts[-1])
    kept = [finish(mine_sum, tokens_last, index) for index in range(CHUNKS)]
    table_grad = table_of(packed, level_table.shape[0])
    result = place_columns(after(y, parts[-1]), half, firsts[:2], kept[:2], received[:2])
    hidden_grad = place_columns(y, half, firsts[2:], kept[2:], received[2:], result)
    return hidden_grad[None], frame_grad[None], table_grad


def solution(mesh):
    staged = mesh.shape["dp"] == 8 and mesh.shape["seq"] == 4
    return jax.shard_map(
        staged_body if staged else plain_body,
        mesh=mesh,
        in_specs=(
            P("dp", "seq", None),
            P("dp", "seq", None),
            P("seq", "dp"),
            P(),
            P(),
            P("dp", "seq"),
            P("dp", None),
        ),
        out_specs=(P("dp", None, "seq"), P("dp", None, "seq"), P("dp", "seq")),
        check_vma=False,
    )
```

```python
import jax
import jax.numpy as jnp
from jax import lax
from jax.experimental import pallas as pl
from jax.experimental.pallas import tpu as pltpu
from jax.sharding import PartitionSpec as P

HIGHEST = lax.Precision.HIGHEST
CHUNKS = 4
BLOCKS = (2, 1, 1)


def onehot(values, count):
    return (values[:, None] == jnp.arange(count, dtype=jnp.int32)[None, :]).astype(jnp.float32)


def gated(grad_out, mod_gate, level_table, frame_ids, levels):
    marks = onehot(levels[0], level_table.shape[0])
    gate_frames = mod_gate[None, :] + jnp.dot(marks, level_table, precision=HIGHEST)
    frames = onehot(frame_ids[0], levels.shape[1])
    gate_tokens = jnp.dot(frames, gate_frames, precision=HIGHEST)
    return (gate_tokens * grad_out[0].astype(jnp.float32)).astype(jnp.bfloat16)


def frame_sums(grad_out, branch_out, frame_ids, levels):
    products = grad_out[0].astype(jnp.float32) * branch_out[0].astype(jnp.float32)
    return jnp.dot(onehot(frame_ids[0], levels.shape[1]).T, products, precision=HIGHEST)


def plain_body(grad_out, branch_out, down_weight, mod_gate, level_table, frame_ids, levels):
    scaled = gated(grad_out, mod_gate, level_table, frame_ids, levels)
    frame_part = frame_sums(grad_out, branch_out, frame_ids, levels)
    hidden_grad = lax.dot_general(
        lax.all_gather(scaled, "seq", axis=0, tiled=True),
        lax.all_gather(down_weight, "dp", axis=1, tiled=True),
        (((1,), (1,)), ((), ())),
        preferred_element_type=jnp.float32,
    ).astype(jnp.bfloat16)
    frame_grad = lax.psum_scatter(frame_part, "seq", scatter_dimension=1, tiled=True)
    marks = onehot(levels[0], level_table.shape[0])
    level_part = jnp.dot(marks.T, frame_grad, precision=HIGHEST)
    table_grad = lax.psum_scatter(level_part, "dp", scatter_dimension=0, tiled=True)
    return hidden_grad[None], frame_grad[None], table_grad


def split_terms(values):
    terms = []
    for _ in range(3):
        term = lax.reduce_precision(values, exponent_bits=8, mantissa_bits=7)
        terms.append(term.astype(jnp.bfloat16))
        values = values - term
    return terms


def with_frame_lines(tokens, frame_part, levels, seq):
    frame_count, width = frame_part.shape
    level_line = jnp.pad(levels.astype(jnp.bfloat16), ((0, 0), (0, width // seq - frame_count)))
    level_line = jnp.tile(level_line, (1, seq))
    lines = jnp.concatenate([*split_terms(frame_part), level_line], axis=0)
    lines = jnp.pad(lines, ((0, -lines.shape[0] % 16), (0, 0)))
    return jnp.concatenate([tokens, lines], axis=0)


def frames_of(me, rows, frame_count, width, pieces):
    lines = pieces[0][0].shape[0] - rows
    any_space = pl.BlockSpec(memory_space=pl.ANY)

    def kernel(place, *refs):
        result, held, sems = refs[8], refs[9], refs[10]
        below = pl.ds(rows, lines)
        columns = pl.ds(pl.multiple_of(place[0] * width, 128), width)
        copies = []
        for ref, (_, index) in zip(refs, pieces):
            source = ref if index is None else ref.at[index]
            copies.append(
                pltpu.make_async_copy(
                    source.at[below, columns], held.at[len(copies)], sems.at[len(copies)]
                )
            )
            copies[-1].start()
        for copy in copies:
            copy.wait()
        for clip in range(2):
            total = jnp.zeros((lines, width), jnp.float32)
            for index in range(4):
                total = total + held[4 * clip + index].astype(jnp.float32)
            sums = total[:frame_count]
            for term in (1, 2):
                sums = sums + total[term * frame_count : (term + 1) * frame_count]
            result[clip, :frame_count] = sums
            marks = held[4 * clip].astype(jnp.float32)
            result[clip, frame_count:] = marks[3 * frame_count : 3 * frame_count + 1]

    return pl.pallas_call(
        kernel,
        out_shape=jax.ShapeDtypeStruct((2, frame_count + 1, width), jnp.float32),
        in_specs=[pl.BlockSpec(memory_space=pltpu.SMEM)] + [any_space] * 8,
        out_specs=pl.BlockSpec(memory_space=pltpu.VMEM),
        scratch_shapes=[
            pltpu.VMEM((8, lines, width), jnp.bfloat16),
            pltpu.SemaphoreType.DMA((8,)),
        ],
        name="frame_lines",
    )(me.astype(jnp.int32).reshape(1), *[array for array, _ in pieces])


def clip_step(packed, dp, flip, gate):
    sent = after(packed, *gate)
    arrived = lax.ppermute(sent, "dp", [(i, i ^ flip) for i in range(dp)])
    return jnp.concatenate([packed, arrived], axis=0)


def table_of(packed, level_count):
    dp, lines, width = packed.shape
    frame_count = lines - 1
    owned = level_count // dp
    rows = (lax.axis_index("dp") * owned + jnp.arange(owned, dtype=jnp.int32)).astype(jnp.float32)
    sums = packed[:, :frame_count].reshape(dp * frame_count, width)
    marks = packed[:, frame_count, :frame_count].reshape(dp * frame_count)
    owners = (rows[:, None] == marks[None, :]).astype(jnp.float32)
    return jnp.dot(owners, sums, precision=HIGHEST)


def after(array, *earlier):
    return lax.optimization_barrier((array, *earlier))[0]


def slice_rows(upper, lower, widths):
    rows = upper.shape[0]
    vmem = pl.BlockSpec(memory_space=pltpu.VMEM)

    def kernel(upper, lower, *results):
        for index, result in enumerate(results):
            chunk = pl.ds(sum(widths[:index]), widths[index])
            result[:rows] = upper[:, chunk]
            result[rows:] = lower[:, chunk]

    return pl.pallas_call(
        kernel,
        out_shape=[jax.ShapeDtypeStruct((2 * rows, width), upper.dtype) for width in widths],
        in_specs=[vmem, vmem],
        out_specs=[vmem] * len(widths),
        compiler_params=pltpu.CompilerParams(vmem_limit_bytes=16 << 20),
        name="slice_rows",
    )(upper, lower)


def block_rows(y, is_mid, blocks):
    rows, width = blocks[0][0].shape
    vmem = pl.BlockSpec(memory_space=pltpu.VMEM)
    parts = [part for block in blocks for part in block]

    def kernel(place, *refs):
        result = refs[len(parts)]
        first = pl.multiple_of(place[0] * rows, 16)
        second = pl.multiple_of((1 - place[0]) * rows, 16)

        def put(block, upper, lower):
            base = 2 * rows * block
            result[pl.ds(pl.multiple_of(base + first, 16), rows), :] = upper[...]
            result[pl.ds(pl.multiple_of(base + second, 16), rows), :] = lower[...]

        index = 0
        for position, block in enumerate(blocks):
            held = refs[index : index + len(block)]
            index += len(block)
            if len(block) == 2:
                put(position, *held)
            else:
                pl.when(place[1] == 1)(lambda: put(position, *held[:2]))
                pl.when(place[1] == 0)(lambda: put(position, *held[2:]))

    return pl.pallas_call(
        kernel,
        out_shape=jax.ShapeDtypeStruct((2 * rows * len(blocks), width), parts[0].dtype),
        in_specs=[pl.BlockSpec(memory_space=pltpu.SMEM)] + [vmem] * len(parts),
        out_specs=vmem,
        compiler_params=pltpu.CompilerParams(vmem_limit_bytes=24 << 20),
        name="block_rows",
    )(jnp.stack([y, is_mid.astype(jnp.int32)]).astype(jnp.int32), *parts)


def last_rows(y, is_mid, width, sent, arrived, offset):
    rows = sent.shape[0] // 2
    vmem = pl.BlockSpec(memory_space=pltpu.VMEM)

    def kernel(place, sent, arrived, result):
        def put(source):
            first = pl.ds(pl.multiple_of(place[0] * rows, 16), rows)
            second = pl.ds(pl.multiple_of((1 - place[0]) * rows, 16), rows)
            result[first, :] = source[:rows, offset : offset + width]
            result[second, :] = source[rows:, offset : offset + width]

        pl.when(place[1] == 1)(lambda: put(sent))
        pl.when(place[1] == 0)(lambda: put(arrived))

    return pl.pallas_call(
        kernel,
        out_shape=jax.ShapeDtypeStruct((2 * rows, width), sent.dtype),
        in_specs=[pl.BlockSpec(memory_space=pltpu.SMEM)] + [vmem] * 2,
        out_specs=vmem,
        compiler_params=pltpu.CompilerParams(vmem_limit_bytes=16 << 20),
        name="last_rows",
    )(jnp.stack([y, is_mid.astype(jnp.int32)]).astype(jnp.int32), sent, arrived)


def order_pieces(me, rows, widths, pieces):
    count, groups = 4, len(widths)
    any_space = pl.BlockSpec(memory_space=pl.ANY)

    def kernel(place, *refs):
        results, sems = refs[count : count + groups], refs[count + groups]
        sources = [
            ref if index is None else ref.at[index] for ref, (_, index) in zip(refs, pieces)
        ]
        copies = []
        for side, width in enumerate(widths):
            columns = pl.ds(sum(widths[:side]), width)
            for flip in range(count):
                start = pl.multiple_of((place[0] ^ flip) * rows, 128)
                source = sources[flip].at[pl.ds(0, rows), columns]
                target = results[side].at[pl.ds(start, rows)]
                copies.append(pltpu.make_async_copy(source, target, sems.at[side * count + flip]))
                copies[-1].start()
        for copy in copies:
            copy.wait()

    return pl.pallas_call(
        kernel,
        out_shape=[
            jax.ShapeDtypeStruct((count * rows, width), pieces[0][0].dtype) for width in widths
        ],
        in_specs=[pl.BlockSpec(memory_space=pltpu.SMEM)] + [any_space] * count,
        out_specs=[pl.BlockSpec(memory_space=pltpu.VMEM)] * groups,
        scratch_shapes=[pltpu.SemaphoreType.DMA((groups * count,))],
        compiler_params=pltpu.CompilerParams(vmem_limit_bytes=16 << 20),
        name="order_pieces",
    )(me.astype(jnp.int32).reshape(1), *[array for array, _ in pieces])


def place_columns(y, half, starts, kept, received, earlier=None):
    count, rows = len(kept), kept[0].shape[0]
    vmem = pl.BlockSpec(memory_space=pltpu.VMEM)
    any_space = pl.BlockSpec(memory_space=pl.ANY)
    held = [] if earlier is None else [earlier]

    def kernel(place, *refs):
        result, sems = refs[2 * count + len(held)], refs[2 * count + len(held) + 1]
        copies = []
        for index, start in enumerate(starts):
            for side, first in ((0, place[0] * half), (1, (1 - place[0]) * half)):
                source = refs[side * count + index]
                column = pl.multiple_of(first + start, 128)
                target = result.at[:, pl.ds(column, source.shape[1])]
                copies.append(
                    pltpu.make_async_copy(source, target, sems.at[2 * index + side])
                )
                copies[-1].start()
        for copy in copies:
            copy.wait()

    return pl.pallas_call(
        kernel,
        out_shape=jax.ShapeDtypeStruct((rows, 2 * half), kept[0].dtype),
        in_specs=[pl.BlockSpec(memory_space=pltpu.SMEM)]
        + [vmem] * (2 * count)
        + [any_space] * len(held),
        out_specs=any_space,
        input_output_aliases={2 * count + 1: 0} if held else {},
        scratch_shapes=[pltpu.SemaphoreType.DMA((2 * count,))],
        compiler_params=pltpu.CompilerParams(vmem_limit_bytes=16 << 20),
        name="place_columns",
    )(y.astype(jnp.int32).reshape(1), *kept, *received, *held)


def staged_body(grad_out, branch_out, down_weight, mod_gate, level_table, frame_ids, levels):
    dp, seq = 8, 4
    clip, me = lax.axis_index("dp"), lax.axis_index("seq")
    z, y = clip // 2, clip % 2
    is_mid = jnp.logical_or(z == 1, z == 2)
    hidden, shard = down_weight.shape
    half = hidden // 2
    block = 2 * shard

    def along_z(array, pairs):
        perm = [(a * 2 + s, b * 2 + s) for a, b in pairs for s in range(2)]
        return lax.ppermute(array, "dp", perm)

    def over_y(array):
        return lax.ppermute(array, "dp", [(i, i ^ 1) for i in range(dp)])

    def over_seq(array, flip):
        return lax.ppermute(array, "seq", [(i, i ^ flip) for i in range(seq)])

    def ordered(flag, first, second, axis):
        swapped = jnp.concatenate([second, first], axis=axis)
        return jnp.where(flag, swapped, jnp.concatenate([first, second], axis=axis))

    weight = down_weight.T
    width = half // CHUNKS
    own_p = lax.dynamic_slice(weight, (0, y * half), (shard, half))
    sent = lax.dynamic_slice(weight, (0, (1 - y) * half), (shard, half))

    scaled = gated(grad_out, mod_gate, level_table, frame_ids, levels)
    frame_part = frame_sums(grad_out, branch_out, frame_ids, levels)
    order = [z, z ^ 1, jnp.where(is_mid, z ^ 3, z ^ 2), jnp.where(is_mid, z ^ 2, z ^ 3)]
    piece = scaled.shape[0]
    scaled = jnp.concatenate(
        [lax.dynamic_slice(scaled, (0, owner * block), (piece, block)) for owner in order], axis=1
    )
    tokens = with_frame_lines(scaled, frame_part, levels, seq)
    def to_near(own):
        return along_z(own, [(0, 1), (1, 0), (2, 3), (3, 2)])

    def across(block):
        return along_z(block, [(1, 2), (2, 1)])

    def outward(block):
        return along_z(block, [(1, 0), (2, 3)])

    own_q = over_y(sent)
    near_p = to_near(own_p)
    crossed_p = across(own_p)

    gate = (own_q, near_p, crossed_p)
    mine_x = over_seq(after(tokens, *gate), 2)
    theirs = over_y(after(tokens, *gate))
    near_q = to_near(after(own_q, *gate))
    crossed_q = across(after(own_q, *gate))
    crossed_near_p = across(after(near_p, *gate))
    forwarded_p = outward(after(crossed_p, *gate, mine_x))

    gate = (near_q, crossed_q, crossed_near_p, forwarded_p)
    theirs_x = over_seq(after(theirs, *gate), 2)
    crossed_near_q = across(after(near_q, *gate))
    forwarded_q = outward(after(crossed_q, *gate))

    own_rows = block_rows(y, is_mid, ((own_p, own_q), (near_p, near_q)))

    gate = (crossed_near_q, forwarded_q, theirs_x)
    three_core = over_seq(after(jnp.stack([tokens, mine_x, theirs]), *gate, own_rows), 1)
    theirs_x_core = over_seq(after(theirs_x, *gate), 1)
    clips = (
        ((tokens, None), (three_core, 0), (mine_x, None), (three_core, 1)),
        ((theirs, None), (three_core, 2), (theirs_x, None), (theirs_x_core, None)),
    )
    cuts = (2 * block, block, block)
    mine = order_pieces(me, piece, cuts, clips[0])
    other = order_pieces(me, piece, cuts, clips[1])
    far = (after(crossed_p, three_core), crossed_q, forwarded_p, forwarded_q)
    far_rows = block_rows(y, is_mid, (far,))

    def first_sum(first, second):
        return jnp.dot(first, own_rows, preferred_element_type=jnp.float32) + jnp.dot(
            second, far_rows, preferred_element_type=jnp.float32
        )

    frame_count = levels.shape[1]
    columns = shard * dp // seq
    packed = frames_of(me, piece, frame_count, columns, clips[0] + clips[1])
    frame_grad = packed[0, :frame_count]
    other_sum = first_sum(other[0], other[1])

    blocks = slice_rows(
        after(crossed_near_p, *gate),
        after(crossed_near_q, *gate),
        [count * width for count in BLOCKS],
    )
    last = [outward(arrived) for arrived in blocks]
    places = [
        (sent, arrived, offset * width)
        for sent, arrived, count in zip(blocks, last, BLOCKS)
        for offset in range(count)
    ]
    firsts = [position * width for position in range(CHUNKS)]
    received, parts, rows = [], [], []

    def finish(earlier, tokens_last, index):
        product = jnp.dot(tokens_last, rows[index], preferred_element_type=jnp.float32)
        return (earlier[:, firsts[index] : firsts[index] + width] + product).astype(jnp.bfloat16)

    for index, (sent, arrived, offset) in enumerate(places):
        if index < 2:
            sent = after(sent, other_sum)
        if index == 2:
            packed = clip_step(packed, dp, 2, (parts[1],))
            sent = after(sent, packed, *parts)
        if index == 3:
            packed = clip_step(packed, dp, 4, (parts[2],))
            sent = after(sent, mine_sum)
        rows.append(last_rows(y, is_mid, width, sent, arrived, offset))
        parts.append(finish(other_sum, other[2], index))
        received.append(over_y(parts[index]))
        if index == 1:
            mine_sum = first_sum(after(mine[0], parts[1]), mine[1])
    tokens_last = after(mine[2], parts[-1])
    kept = [finish(mine_sum, tokens_last, index) for index in range(CHUNKS)]
    table_grad = table_of(packed, level_table.shape[0])
    result = place_columns(after(y, parts[-1]), half, firsts[:2], kept[:2], received[:2])
    hidden_grad = place_columns(y, half, firsts[2:], kept[2:], received[2:], result)
    return hidden_grad[None], frame_grad[None], table_grad


def solution(mesh):
    staged = mesh.shape["dp"] == 8 and mesh.shape["seq"] == 4
    return jax.shard_map(
        staged_body if staged else plain_body,
        mesh=mesh,
        in_specs=(
            P("dp", "seq", None),
            P("dp", "seq", None),
            P("seq", "dp"),
            P(),
            P(),
            P("dp", "seq"),
            P("dp", None),
        ),
        out_specs=(P("dp", None, "seq"), P("dp", None, "seq"), P("dp", "seq")),
        check_vma=False,
    )
```
